32 devices in a mesh: dp: 8 (over z, x), sy: 2 (over y), sx: 2 (over core).
Axes of the slice: x: 2, y: 2, z: 4, core: 2. Of those that a mesh axis runs over, the one named last changes fastest.
Arguments:
- features: bfloat16 [8, 16, 32, 640], P('dp', 'sy', 'sx'), may hold values from -6 to 6
- bucket_ids: int32 [8], P('dp'), may hold values from 0 to 7
- bucket_sizes: int32 [8, 2], replicated, may hold values from 8 to 32, as said below
- conv_weight: bfloat16 [5760, 640], replicated, may hold values from -0.078125 to 0.078125
- norm_gain: float32 [640], replicated, may hold values from 0.25 to 1.75
- query_weight: bfloat16 [640, 640], replicated, may hold values from -0.25 to 0.25
- key_weight: bfloat16 [640, 640], replicated, may hold values from -0.25 to 0.25
- value_weight: bfloat16 [640, 640], replicated, may hold values from -0.25 to 0.25
- out_weight: bfloat16 [640, 640], replicated, may hold values from -0.25 to 0.25
- out_grad: bfloat16 [8, 16, 32, 640], P('dp', 'sy', 'sx'), may hold values from -6 to 6
Outputs:
- block_out: bfloat16 [8, 16, 32, 640], P('dp', 'sy', 'sx')
- grad_conv: float32 [5760, 640], P('dp', ('sy', 'sx'))
- grad_query: float32 [640, 640], P('dp', ('sy', 'sx'))
- grad_key: float32 [640, 640], P('dp', ('sy', 'sx'))
- grad_value: float32 [640, 640], P('dp', ('sy', 'sx'))
- grad_out: float32 [640, 640], P('dp', ('sy', 'sx'))
The draws below stay inside these ranges and needn't reach their ends.
Inputs may be any that keep to these rules, and one draw needn't show every extreme that they name: Each row of bucket_sizes holds a bucket's latent rows, from 8 to 16, and columns, from 16 to 32; bucket 0 is the full 16 x 32 grid and bucket 1 is 8 x 16.
All inputs are finite; a program needn't handle non-finite values.
Results may differ from the reference program's by a relative error of at most 0.013.
Values may be sent and summed in bfloat16 or wider, within the bound.
A program may use at most 192 MiB of HBM per device.

```python
import jax
import jax.numpy as jnp
from jax import lax

C = 640
HEADS = 10
BUCKETS = 8
HG = 16
WG = 32
IMAGES = 8


def draw_bucket_sizes(key, part):
    first = jax.random.fold_in(key, 11)
    second = jax.random.fold_in(key, 23)
    heights = jax.random.randint(first, (BUCKETS, 1), HG // 2, HG + 1, dtype=jnp.int32)
    widths = jax.random.randint(second, (BUCKETS, 1), WG // 2, WG + 1, dtype=jnp.int32)
    sizes = jnp.concatenate([heights, widths], axis=1)
    sizes = sizes.at[0, 0].set(HG).at[0, 1].set(WG)
    sizes = sizes.at[1, 0].set(HG // 2).at[1, 1].set(WG // 2)
    return sizes


def touch_ends(entries, rng, least, largest):
    longest = entries.shape.index(max(entries.shape))
    spots = []
    for shift in (0, 1):
        where = [jax.random.randint(jax.random.fold_in(rng, axis), (), 0, length) for axis, length in enumerate(entries.shape)]
        where[longest] = (where[longest] + shift) % entries.shape[longest]
        spots.append(tuple(where))
    return entries.at[spots[0]].set(least).at[spots[1]].set(largest)


def level_of(stream_key, dims, split, low, high):
    def one(position, blocks):
        steps = jax.random.uniform(jax.random.fold_in(jax.random.fold_in(stream_key, 6), position), (blocks,), jnp.float32, low / len(split), high / len(split))
        return jnp.repeat(jnp.exp(steps), dims[position] // blocks).reshape((-1,) + (1,) * (len(dims) - position - 1))

    loudness = one(*split[0])
    for cut in split[1:]:
        loudness = loudness * one(*cut)
    return loudness


def bell_draw(rng, dims, deviation, limit, pieces=(), kind=jnp.bfloat16):
    level = level_of(rng, dims, pieces, -0.22, 0.18) if pieces else 1.0
    array = jax.random.normal(rng, dims, jnp.float32) * deviation * level
    return jnp.minimum(jnp.maximum(array, -limit), limit).astype(kind)


def setup_inputs(seed: int = 0) -> dict:
    key_of = jax.random.split(jax.random.key(seed), 11)
    return {
        "features": bell_draw(key_of[0], (IMAGES, HG, WG, C), 1.0, 6.0, ((0, 8), (1, 2), (2, 2))),
        "bucket_ids": touch_ends(jax.random.randint(key_of[1], (IMAGES,), 0, BUCKETS), jax.random.fold_in(key_of[1], 1), 0, BUCKETS - 1).astype(jnp.int32),
        "bucket_sizes": draw_bucket_sizes(jax.random.fold_in(key_of[10], 71), 0),
        "conv_weight": bell_draw(key_of[3], (9 * C, C), (9 * C) ** -0.5, 0.078125),
        "norm_gain": jnp.clip(1.0 + 0.15 * jax.random.normal(key_of[4], (C,), jnp.float32), 0.25, 1.75),
        "query_weight": bell_draw(key_of[5], (C, C), C ** -0.5, 0.25),
        "key_weight": bell_draw(key_of[6], (C, C), C ** -0.5, 0.25),
        "value_weight": bell_draw(key_of[7], (C, C), C ** -0.5, 0.25),
        "out_weight": bell_draw(key_of[8], (C, C), C ** -0.5, 0.25),
        "out_grad": bell_draw(key_of[9], (IMAGES, HG, WG, C), 1.0, 6.0, ((0, 8), (1, 2), (2, 2))),
    }


def layer_norm(hidden, gain):
    mean = lax.optimization_barrier(jnp.mean(hidden, axis=-1, keepdims=True))
    centred = hidden - mean
    spread = lax.optimization_barrier(jnp.mean(centred * centred, axis=-1, keepdims=True))
    return centred * lax.rsqrt(spread + 1e-05) * gain.astype(jnp.float32)

def patch_rows(padded, rows, cols):
    taps = [padded[dy:dy + rows, dx:dx + cols, :] for dy in range(3) for dx in range(3)]
    return jnp.concatenate(taps, axis=-1).reshape(rows * cols, -1)

def head_probs(query, keys, key_valid, start, width, scale):
    scores = jnp.dot(query[:, start:start + width], keys[:, start:start + width].T, preferred_element_type=jnp.float32) * scale
    scores = jnp.where(key_valid[None, :], scores, -1e+30)
    return jax.nn.softmax(scores, axis=-1)

def attend(query, keys, values, key_valid, heads):
    width = query.shape[1] // heads
    scale = width ** (-0.5)
    parts = []
    for head in range(heads):
        start = head * width
        probs = head_probs(query, keys, key_valid, start, width, scale)
        parts.append(jnp.dot(probs.astype(jnp.bfloat16), values[:, start:start + width], preferred_element_type=jnp.float32).astype(jnp.bfloat16))
    return jnp.concatenate(parts, axis=-1)

def attend_back(query, keys, values, key_valid, grad_context, heads):
    width = query.shape[1] // heads
    scale = width ** (-0.5)
    dq_parts, dk_parts, dv_parts = ([], [], [])
    for head in range(heads):
        start = head * width
        probs = head_probs(query, keys, key_valid, start, width, scale)
        probs_b = probs.astype(jnp.bfloat16)
        grad_slice = grad_context[:, start:start + width]
        dprob = jnp.dot(grad_slice, values[:, start:start + width].T, preferred_element_type=jnp.float32)
        delta = lax.optimization_barrier(jnp.sum(probs * dprob, axis=-1, keepdims=True))
        dscore = (probs * (dprob - delta) * scale).astype(jnp.bfloat16)
        dq_parts.append(jnp.dot(dscore, keys[:, start:start + width], preferred_element_type=jnp.float32))
        dk_parts.append(jnp.dot(dscore.T, query[:, start:start + width], preferred_element_type=jnp.float32))
        dv_parts.append(jnp.dot(probs_b.T, grad_slice, preferred_element_type=jnp.float32))
    return (jnp.concatenate(dq_parts, axis=-1), jnp.concatenate(dk_parts, axis=-1), jnp.concatenate(dv_parts, axis=-1))

def reference(features, bucket_ids, bucket_sizes, conv_weight, norm_gain, query_weight, key_weight, value_weight, out_weight, out_grad):
    width = features.shape[3]

    def one_image(totals, items):
        feats, bucket, cotangent = items
        chosen = jnp.arange(BUCKETS, dtype=jnp.int32) == bucket
        height = jnp.sum(jnp.where(chosen, bucket_sizes[:, 0], 0))
        breadth = jnp.sum(jnp.where(chosen, bucket_sizes[:, 1], 0))
        valid = (jnp.arange(HG, dtype=jnp.int32)[:, None] < height) & (jnp.arange(WG, dtype=jnp.int32)[None, :] < breadth)
        valid_flat = valid.reshape(-1, 1).astype(jnp.float32)
        key_valid = valid.reshape(-1)
        xin = (feats.astype(jnp.float32) * valid[:, :, None].astype(jnp.float32)).astype(jnp.bfloat16)
        padded = jnp.pad(xin, ((1, 1), (1, 1), (0, 0)))
        patches = patch_rows(padded, HG, WG)
        pre = jnp.dot(patches, conv_weight, preferred_element_type=jnp.float32)
        hidden = (valid_flat * (xin.reshape(-1, width).astype(jnp.float32) + jax.nn.silu(pre))).astype(jnp.bfloat16)
        hidden_f = hidden.astype(jnp.float32)
        normed_f, pullback = jax.vjp(lambda value: layer_norm(value, norm_gain), hidden_f)
        normed = normed_f.astype(jnp.bfloat16)
        query = jnp.dot(normed, query_weight, preferred_element_type=jnp.float32).astype(jnp.bfloat16)
        keys = jnp.dot(normed, key_weight, preferred_element_type=jnp.float32).astype(jnp.bfloat16)
        values = jnp.dot(normed, value_weight, preferred_element_type=jnp.float32).astype(jnp.bfloat16)
        context = attend(query, keys, values, key_valid, HEADS)
        block = (valid_flat * (hidden_f + jnp.dot(context, out_weight, preferred_element_type=jnp.float32))).astype(jnp.bfloat16)
        grad_b = (cotangent.reshape(-1, width).astype(jnp.float32) * valid_flat).astype(jnp.bfloat16)
        grad_wo = jnp.dot(context.T, grad_b, preferred_element_type=jnp.float32)
        grad_context = jnp.dot(grad_b, out_weight.T, preferred_element_type=jnp.float32).astype(jnp.bfloat16)
        dquery, dkey, dvalue = attend_back(query, keys, values, key_valid, grad_context, HEADS)
        dquery = dquery.astype(jnp.bfloat16)
        dkey = dkey.astype(jnp.bfloat16)
        dvalue = dvalue.astype(jnp.bfloat16)
        grad_wq = jnp.dot(normed.T, dquery, preferred_element_type=jnp.float32)
        grad_wk = jnp.dot(normed.T, dkey, preferred_element_type=jnp.float32)
        grad_wv = jnp.dot(normed.T, dvalue, preferred_element_type=jnp.float32)
        dnormed = jnp.dot(dquery, query_weight.T, preferred_element_type=jnp.float32)
        dnormed = dnormed + jnp.dot(dkey, key_weight.T, preferred_element_type=jnp.float32)
        dnormed = dnormed + jnp.dot(dvalue, value_weight.T, preferred_element_type=jnp.float32)
        dhidden = grad_b.astype(jnp.float32) + pullback(dnormed)[0]
        sig = jax.nn.sigmoid(pre)
        dpre = (valid_flat * dhidden * sig * (1.0 + pre * (1.0 - sig))).astype(jnp.bfloat16)
        grad_cv = jnp.dot(patches.T, dpre, preferred_element_type=jnp.float32)
        totals = (totals[0] + grad_cv, totals[1] + grad_wq, totals[2] + grad_wk, totals[3] + grad_wv, totals[4] + grad_wo)
        return (totals, block.reshape(HG, WG, width))
    square = jnp.zeros((width, width), jnp.float32)
    start = (jnp.zeros((9 * width, width), jnp.float32), square, square, square, square)
    totals, blocks = lax.scan(one_image, start, (features, bucket_ids, out_grad))
    return (blocks, totals[0], totals[1], totals[2], totals[3], totals[4])
```

```python
import functools

import jax
import jax.numpy as jnp
from jax import lax
from jax.experimental import pallas as pl
from jax.experimental.pallas import tpu as pltpu
from jax.sharding import PartitionSpec as P

HEADS = 10
F32 = jnp.float32
BF16 = jnp.bfloat16


def layer_norm(hidden, gain):
    mean = jnp.mean(hidden, axis=-1, keepdims=True)
    centred = hidden - mean
    spread = jnp.mean(centred * centred, axis=-1, keepdims=True)
    return centred * lax.rsqrt(spread + 1e-05) * gain


def patch_rows(padded, rows, cols):
    taps = [padded[dy : dy + rows, dx : dx + cols, :] for dy in range(3) for dx in range(3)]
    return jnp.concatenate(taps, axis=-1).reshape(rows * cols, -1)


def dot_t(a, b, ca, cb):
    return lax.dot_general(a, b, (((ca,), (cb,)), ((), ())), preferred_element_type=F32)


def attention_kernel(width, valid_ref, q_ref, k_ref, v_ref, g_ref, c_ref, dq_ref, dk_ref, dv_ref):
    scale = width ** (-0.5)
    mask = valid_ref[...] > 0.0
    parts = ([], [], [], [])
    for start in range(0, q_ref.shape[1], width):
        q = q_ref[:, start : start + width]
        k = k_ref[:, start : start + width]
        v = v_ref[:, start : start + width]
        g = g_ref[:, start : start + width]
        scores = jnp.where(mask, dot_t(q, k, 1, 1) * scale, -1e30)
        expo = jnp.exp(scores - jnp.max(scores, axis=-1, keepdims=True))
        probs = expo * (1.0 / jnp.sum(expo, axis=-1, keepdims=True))
        probs_b = probs.astype(BF16)
        dprob = dot_t(g, v, 1, 1)
        delta = jnp.sum(probs * dprob, axis=-1, keepdims=True)
        dscore = (probs * (dprob - delta) * scale).astype(BF16)
        parts[0].append(dot_t(probs_b, v, 1, 0))
        parts[1].append(dot_t(dscore, k, 1, 0))
        parts[2].append(dot_t(dscore, q, 0, 0))
        parts[3].append(dot_t(probs_b, g, 0, 0))
    for ref, part in zip((c_ref, dq_ref, dk_ref, dv_ref), parts):
        ref[...] = jnp.concatenate(part, axis=-1).astype(BF16)


def attention(valid_row, query, keys, values, grads, heads):
    cells, channels = query.shape
    width = channels // heads
    block = pl.BlockSpec((cells, 2 * width), lambda i: (0, i))
    shape = jax.ShapeDtypeStruct((cells, channels), BF16)
    return pl.pallas_call(
        functools.partial(attention_kernel, width),
        grid=(heads // 2,),
        in_specs=[pl.BlockSpec((1, cells), lambda i: (0, 0))] + [block] * 4,
        out_specs=[block] * 4,
        out_shape=[shape] * 4,
        compiler_params=pltpu.CompilerParams(vmem_limit_bytes=48 * 1024 * 1024),
        cost_estimate=pl.CostEstimate(
            flops=12 * cells * cells * channels,
            bytes_accessed=16 * cells * channels,
            transcendentals=heads * cells * cells,
        ),
    )(valid_row, query, keys, values, grads)


def exchange_kernel(count, a_ref, b_ref, a_out, b_out, a_got, b_got, send_sem, recv_sem):
    me = lax.axis_index("dp")
    barrier = pltpu.get_barrier_semaphore()
    for step in range(1, count):
        pl.semaphore_signal(
            barrier,
            inc=1,
            device_id={"dp": lax.rem(me + step, count)},
            device_id_type=pl.DeviceIdType.MESH,
        )
    pl.semaphore_wait(barrier, count - 1)
    copies = []
    for which, (src, got) in enumerate(((a_ref, a_got), (b_ref, b_got))):
        for step in range(1, count):
            peer = lax.rem(me + step, count)
            copy = pltpu.make_async_remote_copy(
                src_ref=src.at[peer],
                dst_ref=got.at[step - 1],
                send_sem=send_sem.at[which, step - 1],
                recv_sem=recv_sem.at[which, step - 1],
                device_id={"dp": peer},
                device_id_type=pl.DeviceIdType.MESH,
            )
            copy.start()
            copies.append(copy)
    a_out[...] = a_ref[me].astype(F32)
    b_out[...] = b_ref[me].astype(F32)
    for index, copy in enumerate(copies):
        copy.wait_recv()
        step = index % (count - 1)
        if index < count - 1:
            a_out[...] += a_got[step].astype(F32)
        else:
            b_out[...] += b_got[step].astype(F32)
    for copy in copies:
        copy.wait_send()


def exchange(a, b):
    count = a.shape[0]
    vmem = pl.BlockSpec(memory_space=pltpu.VMEM)
    return pl.pallas_call(
        functools.partial(exchange_kernel, count),
        in_specs=[vmem, vmem],
        out_specs=[vmem, vmem],
        out_shape=[
            jax.ShapeDtypeStruct(a.shape[1:], F32),
            jax.ShapeDtypeStruct(b.shape[1:], F32),
        ],
        scratch_shapes=[
            pltpu.VMEM((count - 1,) + a.shape[1:], BF16),
            pltpu.VMEM((count - 1,) + b.shape[1:], BF16),
            pltpu.SemaphoreType.DMA((2, count - 1)),
            pltpu.SemaphoreType.DMA((2, count - 1)),
        ],
        compiler_params=pltpu.CompilerParams(
            collective_id=0, has_side_effects=True, vmem_limit_bytes=48 * 1024 * 1024
        ),
    )(a, b)


def body(
    features,
    bucket_ids,
    bucket_sizes,
    conv_weight,
    norm_gain,
    query_weight,
    key_weight,
    value_weight,
    out_weight,
    out_grad,
):
    rows_dev, cols_dev, width = features.shape[1:]
    count_y = lax.axis_size("sy")
    count_x = lax.axis_size("sx")
    count_d = lax.axis_size("dp")
    at_y, at_x = lax.axis_index("sy"), lax.axis_index("sx")
    rows, cols = rows_dev * count_y, cols_dev * count_x
    cells = rows * cols
    share = width // (count_y * count_x)
    first = (at_y * count_x + at_x) * share
    chosen = jnp.arange(bucket_sizes.shape[0], dtype=jnp.int32) == bucket_ids[0]
    height = jnp.sum(jnp.where(chosen, bucket_sizes[:, 0], 0))
    breadth = jnp.sum(jnp.where(chosen, bucket_sizes[:, 1], 0))
    valid = (jnp.arange(rows, dtype=jnp.int32)[:, None] < height) & (
        jnp.arange(cols, dtype=jnp.int32)[None, :] < breadth
    )
    valid_flat = valid.reshape(-1, 1).astype(F32)

    both = lax.all_gather(
        jnp.stack([features[0], out_grad[0]]), ("sy", "sx"), axis=0, tiled=False
    )
    both = both.reshape(count_y, count_x, 2, rows_dev, cols_dev, width)
    both = both.transpose(2, 0, 3, 1, 4, 5).reshape(2, rows, cols, width)
    both = jnp.where(valid[None, :, :, None], both, jnp.zeros((), BF16))
    xin = both[0]
    grad_b = both[1].reshape(cells, width)

    patches = patch_rows(jnp.pad(xin, ((1, 1), (1, 1), (0, 0))), rows, cols)
    pre = jnp.dot(patches, conv_weight, preferred_element_type=F32)
    hidden = (valid_flat * (xin.reshape(cells, width).astype(F32) + jax.nn.silu(pre))).astype(BF16)
    normed_f, pullback = jax.vjp(lambda value: layer_norm(value, norm_gain), hidden.astype(F32))
    normed = normed_f.astype(BF16)
    query = jnp.dot(normed, query_weight, preferred_element_type=F32).astype(BF16)
    keys = jnp.dot(normed, key_weight, preferred_element_type=F32).astype(BF16)
    values = jnp.dot(normed, value_weight, preferred_element_type=F32).astype(BF16)
    grad_context = dot_t(grad_b, out_weight, 1, 1).astype(BF16)
    context, dquery, dkey, dvalue = attention(
        valid_flat.reshape(1, cells), query, keys, values, grad_context, HEADS
    )

    def own_cells(array):
        grid = array.reshape(rows, cols, -1)
        tile = lax.dynamic_slice(
            grid,
            (at_y * rows_dev, at_x * cols_dev, 0),
            (rows_dev, cols_dev, grid.shape[2]),
        )
        return tile.reshape(rows_dev * cols_dev, -1)

    def own_columns(array):
        return lax.dynamic_slice_in_dim(array, first, share, axis=1)

    block = (
        own_cells(valid_flat)
        * (
            own_cells(hidden).astype(F32)
            + jnp.dot(own_cells(context), out_weight, preferred_element_type=F32)
        )
    ).astype(BF16)

    dthree = jnp.concatenate(
        [own_columns(dquery), own_columns(dkey), own_columns(dvalue)], axis=1
    )
    squares = jnp.concatenate(
        [dot_t(normed, dthree, 0, 0), dot_t(context, own_columns(grad_b), 0, 0)], axis=1
    ).astype(BF16)
    squares = squares.reshape(count_d, width // count_d, 4 * share)

    dnormed = (
        dot_t(dquery, query_weight, 1, 1)
        + dot_t(dkey, key_weight, 1, 1)
        + dot_t(dvalue, value_weight, 1, 1)
    )
    dhidden = grad_b.astype(F32) + pullback(dnormed)[0]
    sig = jax.nn.sigmoid(pre)
    dpre = (valid_flat * dhidden * sig * (1.0 + pre * (1.0 - sig))).astype(BF16)
    dpre_t = lax.dynamic_slice_in_dim(dpre.T, first, share, axis=0)
    piece = patches.shape[1] // count_d
    lanes = -(-piece // 128) * 128
    conv_t = jnp.dot(dpre_t, patches, preferred_element_type=F32).astype(BF16)
    conv_t = conv_t.reshape(share, count_d, piece).transpose(1, 0, 2)
    conv_t = jnp.pad(conv_t, ((0, 0), (0, 0), (0, lanes - piece)))

    conv_sum, square_sum = exchange(conv_t, squares)
    grad_cv = conv_sum[:, :piece].T
    grads = [square_sum[:, i * share : (i + 1) * share] for i in range(4)]
    return (block.reshape(1, rows_dev, cols_dev, width), grad_cv, *grads)


def solution(mesh):
    placed = (
        P("dp", "sy", "sx", None),
        P("dp"),
        P(),
        P(),
        P(),
        P(),
        P(),
        P(),
        P(),
        P("dp", "sy", "sx", None),
    )
    return jax.shard_map(
        body,
        mesh=mesh,
        in_specs=placed,
        out_specs=(
            P("dp", "sy", "sx", None),
            P("dp", ("sy", "sx")),
            P("dp", ("sy", "sx")),
            P("dp", ("sy", "sx")),
            P("dp", ("sy", "sx")),
            P("dp", ("sy", "sx")),
        ),
        check_vma=False,
    )
```

```python
import functools

import jax
import jax.numpy as jnp
from jax import lax
from jax.experimental import pallas as pl
from jax.experimental.pallas import tpu as pltpu
from jax.sharding import PartitionSpec as P

HEADS = 10
F32 = jnp.float32
BF16 = jnp.bfloat16


VMEM_LIMIT = 56 * 1024 * 1024
MESH = pl.DeviceIdType.MESH


def dot_t(a, b, ca, cb):
    return lax.dot_general(a, b, (((ca,), (cb,)), ((), ())), preferred_element_type=F32)


def attention_kernel(width, valid_ref, q_ref, k_ref, v_ref, g_ref, c_ref, dq_ref, dk_ref, dv_ref):
    scale = width ** (-0.5)
    mask = valid_ref[...] > 0.0
    parts = ([], [], [], [])
    for start in range(0, q_ref.shape[1], width):
        q = q_ref[:, start : start + width]
        k = k_ref[:, start : start + width]
        v = v_ref[:, start : start + width]
        g = g_ref[:, start : start + width]
        scores = jnp.where(mask, dot_t(q, k, 1, 1) * scale, -1e30)
        expo = jnp.exp(scores - jnp.max(scores, axis=-1, keepdims=True))
        probs = expo * (1.0 / jnp.sum(expo, axis=-1, keepdims=True))
        probs_b = probs.astype(BF16)
        dprob = dot_t(g, v, 1, 1)
        delta = jnp.sum(probs * dprob, axis=-1, keepdims=True)
        dscore = (probs * (dprob - delta) * scale).astype(BF16)
        parts[0].append(dot_t(probs_b, v, 1, 0))
        parts[1].append(dot_t(dscore, k, 1, 0))
        parts[2].append(dot_t(dscore, q, 0, 0))
        parts[3].append(dot_t(probs_b, g, 0, 0))
    for ref, part in zip((c_ref, dq_ref, dk_ref, dv_ref), parts):
        ref[...] = jnp.concatenate(part, axis=-1).astype(BF16)


def attention(valid_row, query, keys, values, grads, heads):
    cells, channels = query.shape
    width = channels // heads
    block = pl.BlockSpec((cells, 2 * width), lambda i: (0, i))
    shape = jax.ShapeDtypeStruct((cells, channels), BF16)
    return pl.pallas_call(
        functools.partial(attention_kernel, width),
        grid=(heads // 2,),
        in_specs=[pl.BlockSpec((1, cells), lambda i: (0, 0))] + [block] * 4,
        out_specs=[block] * 4,
        out_shape=[shape] * 4,
        compiler_params=pltpu.CompilerParams(vmem_limit_bytes=48 * 1024 * 1024),
        cost_estimate=pl.CostEstimate(
            flops=12 * cells * cells * channels,
            bytes_accessed=16 * cells * channels,
            transcendentals=heads * cells * cells,
        ),
    )(valid_row, query, keys, values, grads)


def front_kernel(
    f_ref, g_ref, w_ref, valid_ref, gain_ref,
    s_ref, gb_ref, pre_ref, hid_ref, norm_ref,
    grid, weight, w_sem, own_sem, y_send, y_recv, x_send, x_recv,
):
    count_y, count_x = lax.axis_size("sy"), lax.axis_size("sx")
    at_y, at_x = lax.axis_index("sy"), lax.axis_index("sx")
    rows_dev, cols_dev, width = f_ref.shape
    rows, cols = grid.shape[1:3]
    cells = rows * cols
    barrier = pltpu.get_barrier_semaphore()
    for step in range(1, count_y):
        pl.semaphore_signal(
            barrier, inc=1, device_id={"sy": lax.rem(at_y + step, count_y)}, device_id_type=MESH
        )
    for step in range(1, count_x):
        pl.semaphore_signal(
            barrier, inc=1, device_id={"sx": lax.rem(at_x + step, count_x)}, device_id_type=MESH
        )
    pl.semaphore_wait(barrier, count_y + count_x - 2)

    def tile(which, y):
        return grid.at[
            which,
            pl.ds(y * rows_dev, rows_dev),
            pl.ds(pl.multiple_of(at_x * cols_dev, cols_dev), cols_dev),
        ]

    fetch = pltpu.make_async_copy(w_ref, weight, w_sem)
    locals_, ups, acrosses = [], [[], []], [[], []]
    for which, ref in enumerate((f_ref, g_ref)):
        for step in range(1, count_y):
            copy = pltpu.make_async_remote_copy(
                src_ref=ref,
                dst_ref=tile(which, at_y),
                send_sem=y_send.at[which, step - 1],
                recv_sem=y_recv.at[which, step - 1],
                device_id={"sy": lax.rem(at_y + step, count_y)},
                device_id_type=MESH,
            )
            copy.start()
            ups[which].append(copy)
        own = pltpu.make_async_copy(ref, tile(which, at_y), own_sem.at[which])
        own.start()
        locals_.append(own)
    fetch.start()

    def across(which, back):
        y = lax.rem(at_y - back + count_y, count_y)
        for step in range(1, count_x):
            copy = pltpu.make_async_remote_copy(
                src_ref=(f_ref, g_ref)[which] if back == 0 else tile(which, y),
                dst_ref=tile(which, y),
                send_sem=x_send.at[which, back, step - 1],
                recv_sem=x_recv.at[which, back, step - 1],
                device_id={"sx": lax.rem(at_x + step, count_x)},
                device_id_type=MESH,
            )
            copy.start()
            acrosses[which].append(copy)

    across(0, 0)
    across(1, 0)
    for back in range(1, count_y):
        ups[0][back - 1].wait_recv()
        across(0, back)
    locals_[0].wait()
    for copy in acrosses[0]:
        copy.wait_recv()

    edge = jnp.zeros((cols, width), BF16)
    for shift in range(3):
        s_ref[shift, 0:cols, :] = edge
        s_ref[shift, cells + cols : cells + 2 * cols, :] = edge

    def build(r, carry):
        at = pl.ds(pl.multiple_of(r * cols, cols), cols)
        to = pl.ds(pl.multiple_of((r + 1) * cols, cols), cols)
        line = grid[0, r].astype(F32) * valid_ref[at, :]
        zero = jnp.zeros((1, width), F32)
        s_ref[0, to, :] = jnp.concatenate([zero, line[:-1]], axis=0).astype(BF16)
        s_ref[1, to, :] = line.astype(BF16)
        s_ref[2, to, :] = jnp.concatenate([line[1:], zero], axis=0).astype(BF16)
        return carry

    lax.fori_loop(0, rows, build, 0)
    for back in range(1, count_y):
        ups[1][back - 1].wait_recv()
        across(1, back)
    fetch.wait()

    def tap(t, carry):
        dy, dx = t // 3, t % 3
        part = jnp.dot(
            s_ref[dx, pl.ds(pl.multiple_of(dy * cols, cols), cells), :],
            weight[pl.ds(pl.multiple_of(t * width, width), width), :],
            preferred_element_type=F32,
        )
        pre_ref[...] += part
        return carry

    pre_ref[...] = jnp.zeros_like(pre_ref)
    lax.fori_loop(0, 9, tap, 0)
    locals_[1].wait()
    for copy in acrosses[1]:
        copy.wait_recv()

    def finish(r, carry):
        at = pl.ds(pl.multiple_of(r * cols, cols), cols)
        valid = valid_ref[at, :]
        gb_ref[at, :] = (grid[1, r].astype(F32) * valid).astype(BF16)
        pre = pre_ref[at, :]
        xin = s_ref[1, pl.ds(pl.multiple_of((r + 1) * cols, cols), cols), :].astype(F32)
        hidden = (valid * (xin + pre * jax.nn.sigmoid(pre))).astype(BF16)
        hid_ref[at, :] = hidden
        hidden = hidden.astype(F32)
        centred = hidden - jnp.mean(hidden, axis=-1, keepdims=True)
        spread = jnp.mean(centred * centred, axis=-1, keepdims=True)
        norm_ref[at, :] = (centred * lax.rsqrt(spread + 1e-05) * gain_ref[...]).astype(BF16)
        return carry

    lax.fori_loop(0, rows, finish, 0)
    for group in ups + acrosses:
        for copy in group:
            copy.wait_send()


def front(features, out_grad, conv_weight, valid, gain):
    count_y, count_x = lax.axis_size("sy"), lax.axis_size("sx")
    rows_dev, cols_dev, width = features.shape
    rows, cols = rows_dev * count_y, cols_dev * count_x
    cells = rows * cols
    vmem = pl.BlockSpec(memory_space=pltpu.VMEM)
    anywhere = pl.BlockSpec(memory_space=pl.ANY)
    dma = pltpu.SemaphoreType.DMA
    return pl.pallas_call(
        front_kernel,
        in_specs=[anywhere, anywhere, anywhere, vmem, vmem],
        out_specs=[vmem] * 5,
        out_shape=[
            jax.ShapeDtypeStruct((3, cells + 2 * cols, width), BF16),
            jax.ShapeDtypeStruct((cells, width), BF16),
            jax.ShapeDtypeStruct((cells, width), F32),
            jax.ShapeDtypeStruct((cells, width), BF16),
            jax.ShapeDtypeStruct((cells, width), BF16),
        ],
        scratch_shapes=[
            pltpu.VMEM((2, rows, cols, width), BF16),
            pltpu.VMEM(conv_weight.shape, BF16),
            dma,
            dma((2,)),
            dma((2, count_y - 1)),
            dma((2, count_y - 1)),
            dma((2, count_y, count_x - 1)),
            dma((2, count_y, count_x - 1)),
        ],
        compiler_params=pltpu.CompilerParams(
            collective_id=1, has_side_effects=True, vmem_limit_bytes=VMEM_LIMIT
        ),
    )(features, out_grad, conv_weight, valid, gain)


def back_kernel(
    share, sq_ref, dq_ref, dk_ref, dv_ref, wq_ref, wk_ref, wv_ref, wo_ref,
    gb_ref, hid_ref, pre_ref, ctx_ref, valid_ref, gain_ref, s_ref,
    cv_out, sq_out, block_out,
    own, own_t, taps, cv, cv_pair, sq_pair, cv_sum, sq_sum, cv_got, sq_got,
    pair_send, pair_recv, far_send, far_recv,
):
    count = lax.axis_size("dp")
    half = count // 2
    me = lax.axis_index("dp")
    level, bit = me // 2, me % 2
    partner = me + 1 - 2 * bit
    at_y, at_x = lax.axis_index("sy"), lax.axis_index("sx")
    place = at_y * lax.axis_size("sx") + at_x
    cells, width = gb_ref.shape
    cols = s_ref.shape[1] - cells
    cols = cols // 2
    barrier = pltpu.get_barrier_semaphore()
    pl.semaphore_signal(barrier, inc=1, device_id={"dp": partner}, device_id_type=MESH)
    for step in range(1, half):
        pl.semaphore_signal(
            barrier,
            inc=1,
            device_id={"dp": 2 * lax.rem(level + step, half) + bit},
            device_id_type=MESH,
        )
    pl.semaphore_wait(barrier, half)

    order = list(range(1, half)) + [0]

    def to_partner(which, src, got):
        copies = {}
        for step in order:
            chunk = 2 * lax.rem(level + step, half) + 1 - bit
            copies[step] = pltpu.make_async_remote_copy(
                src_ref=src.at[chunk],
                dst_ref=got.at[step],
                send_sem=pair_send.at[which, step],
                recv_sem=pair_recv.at[which, step],
                device_id={"dp": partner},
                device_id_type=MESH,
            )
            copies[step].start()
        return copies

    def to_far(which, near, src, got, total, landed):
        copies = {}
        for step in order[:-1]:
            peer = 2 * lax.rem(level + step, half) + bit
            near[step].wait_recv()
            total[step - 1] = (src[peer].astype(F32) + got[step].astype(F32)).astype(BF16)
            copies[step] = pltpu.make_async_remote_copy(
                src_ref=total.at[step - 1],
                dst_ref=landed.at[step - 1],
                send_sem=far_send.at[which, step - 1],
                recv_sem=far_recv.at[which, step - 1],
                device_id={"dp": peer},
                device_id_type=MESH,
            )
            copies[step].start()
        return copies

    def collect(near, far, src, got, landed, out):
        near[0].wait_recv()
        value = src[me].astype(F32) + got[0].astype(F32)
        for step in order[:-1]:
            far[step].wait_recv()
            value += landed[step - 1].astype(F32)
        out[...] = value

    sq_near = to_partner(0, sq_ref, sq_pair)

    rows_at = cells // 4

    def backward(r, carry):
        at = pl.ds(pl.multiple_of(r * rows_at, rows_at), rows_at)
        dnormed = dot_t(dq_ref[at, :], wq_ref[...], 1, 1)
        dnormed += dot_t(dk_ref[at, :], wk_ref[...], 1, 1)
        dnormed += dot_t(dv_ref[at, :], wv_ref[...], 1, 1)
        hidden = hid_ref[at, :].astype(F32)
        centred = hidden - jnp.mean(hidden, axis=-1, keepdims=True)
        spread = jnp.mean(centred * centred, axis=-1, keepdims=True)
        rstd = lax.rsqrt(spread + 1e-05)
        unit = centred * rstd
        up = dnormed * gain_ref[...]
        down = up - jnp.mean(up, axis=-1, keepdims=True)
        down = rstd * (down - unit * jnp.mean(up * unit, axis=-1, keepdims=True))
        pre = pre_ref[at, :]
        sig = jax.nn.sigmoid(pre)
        dpre = (gb_ref[at, :].astype(F32) + down) * sig * (1.0 + pre * (1.0 - sig))
        dpre = dpre * valid_ref[at, :]
        mine = dpre[:, 0:share]
        for index in range(1, width // share):
            mine = jnp.where(place == index, dpre[:, index * share : (index + 1) * share], mine)
        own[at, :] = mine
        return carry

    lax.fori_loop(0, 4, backward, 0)
    sq_far = to_far(0, sq_near, sq_ref, sq_pair, sq_sum, sq_got)
    own_t[...] = own[...].T.astype(BF16)
    for t in range(9):
        dy, dx = t // 3, t % 3
        taps[:, t * width : (t + 1) * width] = jnp.dot(
            own_t[...],
            s_ref[dx, dy * cols : dy * cols + cells, :],
            preferred_element_type=F32,
        )
    piece = taps.shape[1] // count
    spare = jnp.zeros((share, cv.shape[2] - piece), F32)
    for index in range(count):
        part = taps[:, index * piece : (index + 1) * piece]
        cv[index] = jnp.concatenate([part, spare], axis=1).astype(BF16)
    cv_near = to_partner(1, cv, cv_pair)

    rows_dev, cols_dev = block_out.shape[:2]
    rows_own = pl.ds(at_y * rows_dev, rows_dev)
    cols_own = pl.ds(pl.multiple_of(at_x * cols_dev, cols_dev), cols_dev)
    context = ctx_ref[rows_own, cols_own, :].reshape(rows_dev * cols_dev, width)
    made = jnp.dot(context, wo_ref[...], preferred_element_type=F32)
    for r in range(rows_dev):
        start = pl.multiple_of((at_y * rows_dev + r) * cols + at_x * cols_dev, cols_dev)
        line = pl.ds(start, cols_dev)
        value = hid_ref[line, :].astype(F32) + made[r * cols_dev : (r + 1) * cols_dev]
        block_out[r] = (value * valid_ref[line, :]).astype(BF16)

    cv_far = to_far(1, cv_near, cv, cv_pair, cv_sum, cv_got)
    collect(sq_near, sq_far, sq_ref, sq_pair, sq_got, sq_out)
    collect(cv_near, cv_far, cv, cv_pair, cv_got, cv_out)
    for group in (sq_near, sq_far, cv_near, cv_far):
        for copy in group.values():
            copy.wait_send()


def back(share, tile_shape, squares, arrays, context_grid, valid, gain, stack, piece):
    count = squares.shape[0]
    half = count // 2
    cells, width = arrays[0].shape
    lanes = -(-piece // 128) * 128
    vmem = pl.BlockSpec(memory_space=pltpu.VMEM)
    dma = pltpu.SemaphoreType.DMA
    conv_shape, square_shape = (share, lanes), squares.shape[1:]
    return pl.pallas_call(
        functools.partial(back_kernel, share),
        in_specs=[vmem] * 15,
        out_specs=[vmem] * 3,
        out_shape=[
            jax.ShapeDtypeStruct(conv_shape, F32),
            jax.ShapeDtypeStruct(square_shape, F32),
            jax.ShapeDtypeStruct(tile_shape, BF16),
        ],
        scratch_shapes=[
            pltpu.VMEM((cells, share), F32),
            pltpu.VMEM((share, cells), BF16),
            pltpu.VMEM((share, 9 * width), F32),
            pltpu.VMEM((count,) + conv_shape, BF16),
            pltpu.VMEM((half,) + conv_shape, BF16),
            pltpu.VMEM((half,) + square_shape, BF16),
            pltpu.VMEM((half - 1,) + conv_shape, BF16),
            pltpu.VMEM((half - 1,) + square_shape, BF16),
            pltpu.VMEM((half - 1,) + conv_shape, BF16),
            pltpu.VMEM((half - 1,) + square_shape, BF16),
            dma((2, half)),
            dma((2, half)),
            dma((2, half - 1)),
            dma((2, half - 1)),
        ],
        compiler_params=pltpu.CompilerParams(
            collective_id=2, has_side_effects=True, vmem_limit_bytes=VMEM_LIMIT
        ),
    )(squares, *arrays, context_grid, valid, gain, stack)


def body(
    features,
    bucket_ids,
    bucket_sizes,
    conv_weight,
    norm_gain,
    query_weight,
    key_weight,
    value_weight,
    out_weight,
    out_grad,
):
    rows_dev, cols_dev, width = features.shape[1:]
    count_y = lax.axis_size("sy")
    count_x = lax.axis_size("sx")
    count_d = lax.axis_size("dp")
    at_y, at_x = lax.axis_index("sy"), lax.axis_index("sx")
    rows, cols = rows_dev * count_y, cols_dev * count_x
    cells = rows * cols
    share = width // (count_y * count_x)
    first = (at_y * count_x + at_x) * share
    chosen = jnp.arange(bucket_sizes.shape[0], dtype=jnp.int32) == bucket_ids[0]
    height = jnp.sum(jnp.where(chosen, bucket_sizes[:, 0], 0))
    breadth = jnp.sum(jnp.where(chosen, bucket_sizes[:, 1], 0))
    valid = (jnp.arange(rows, dtype=jnp.int32)[:, None] < height) & (
        jnp.arange(cols, dtype=jnp.int32)[None, :] < breadth
    )
    valid_flat = valid.reshape(-1, 1).astype(F32)
    gain = norm_gain.reshape(1, width)

    stack, grad_b, pre, hidden, normed = front(
        features[0], out_grad[0], conv_weight, valid_flat, gain
    )
    query = jnp.dot(normed, query_weight, preferred_element_type=F32).astype(BF16)
    keys = jnp.dot(normed, key_weight, preferred_element_type=F32).astype(BF16)
    values = jnp.dot(normed, value_weight, preferred_element_type=F32).astype(BF16)
    grad_context = dot_t(grad_b, out_weight, 1, 1).astype(BF16)
    context, dquery, dkey, dvalue = attention(
        valid_flat.reshape(1, cells), query, keys, values, grad_context, HEADS
    )

    def own_columns(array):
        return lax.dynamic_slice_in_dim(array, first, share, axis=1)

    dthree = jnp.concatenate(
        [own_columns(dquery), own_columns(dkey), own_columns(dvalue)], axis=1
    )
    squares = jnp.concatenate(
        [dot_t(normed, dthree, 0, 0), dot_t(context, own_columns(grad_b), 0, 0)], axis=1
    ).astype(BF16)
    squares = squares.reshape(count_d, width // count_d, 4 * share)
    piece = conv_weight.shape[0] // count_d
    conv_sum, square_sum, block = back(
        share,
        features.shape[1:],
        squares,
        (dquery, dkey, dvalue, query_weight, key_weight, value_weight, out_weight,
         grad_b, hidden, pre),
        context.reshape(rows, cols, width),
        valid_flat,
        gain,
        stack,
        piece,
    )
    grad_cv = conv_sum[:, :piece].T
    grads = [square_sum[:, i * share : (i + 1) * share] for i in range(4)]
    return (block[None], grad_cv, *grads)


def solution(mesh):
    placed = (
        P("dp", "sy", "sx", None),
        P("dp"),
        P(),
        P(),
        P(),
        P(),
        P(),
        P(),
        P(),
        P("dp", "sy", "sx", None),
    )
    return jax.shard_map(
        body,
        mesh=mesh,
        in_specs=placed,
        out_specs=(
            P("dp", "sy", "sx", None),
            P("dp", ("sy", "sx")),
            P("dp", ("sy", "sx")),
            P("dp", ("sy", "sx")),
            P("dp", ("sy", "sx")),
            P("dp", ("sy", "sx")),
        ),
        check_vma=False,
    )
```

```python
import functools

import jax
import jax.numpy as jnp
from jax import lax
from jax.experimental import pallas as pl
from jax.experimental.pallas import tpu as pltpu
from jax.sharding import PartitionSpec as P

HEADS = 10
F32 = jnp.float32
BF16 = jnp.bfloat16


VMEM_LIMIT = 56 * 1024 * 1024
MESH = pl.DeviceIdType.MESH


def dot_t(a, b, ca, cb):
    return lax.dot_general(a, b, (((ca,), (cb,)), ((), ())), preferred_element_type=F32)


def bucket_size(ids_ref, sizes_ref):
    height, breadth = jnp.int32(0), jnp.int32(0)
    for index in range(sizes_ref.shape[0]):
        height = jnp.where(ids_ref[0] == index, sizes_ref[index, 0], height)
        breadth = jnp.where(ids_ref[0] == index, sizes_ref[index, 1], breadth)
    return height, breadth


def attention_kernel(
    width, cols, ids_ref, sizes_ref, n_ref, gb_ref, wq_ref, wk_ref, wv_ref, wo_ref,
    c_ref, dq_ref, dk_ref, dv_ref,
):
    scale = width ** (-0.5)
    height, breadth = bucket_size(ids_ref, sizes_ref)
    index = lax.broadcasted_iota(jnp.int32, (1, n_ref.shape[0]), 1)
    mask = (index // cols < height) & (index % cols < breadth)
    normed = n_ref[...]
    q_both = jnp.dot(normed, wq_ref[...], preferred_element_type=F32).astype(BF16)
    k_both = jnp.dot(normed, wk_ref[...], preferred_element_type=F32).astype(BF16)
    v_both = jnp.dot(normed, wv_ref[...], preferred_element_type=F32).astype(BF16)
    g_both = dot_t(gb_ref[...], wo_ref[...], 1, 1).astype(BF16)
    parts = ([], [], [], [])
    for start in range(0, q_both.shape[1], width):
        q = q_both[:, start : start + width]
        k = k_both[:, start : start + width]
        v = v_both[:, start : start + width]
        g = g_both[:, start : start + width]
        scores = jnp.where(mask, dot_t(q, k, 1, 1) * scale, -1e30)
        expo = jnp.exp(scores - jnp.max(scores, axis=-1, keepdims=True))
        probs = expo * (1.0 / jnp.sum(expo, axis=-1, keepdims=True))
        probs_b = probs.astype(BF16)
        dprob = dot_t(g, v, 1, 1)
        delta = jnp.sum(probs * dprob, axis=-1, keepdims=True)
        dscore = (probs * (dprob - delta) * scale).astype(BF16)
        parts[0].append(dot_t(probs_b, v, 1, 0))
        parts[1].append(dot_t(dscore, k, 1, 0))
        parts[2].append(dot_t(dscore, q, 0, 0))
        parts[3].append(dot_t(probs_b, g, 0, 0))
    for ref, part in zip((c_ref, dq_ref, dk_ref, dv_ref), parts):
        ref[...] = jnp.concatenate(part, axis=-1).astype(BF16)


def attention(ids, sizes, normed, grad_b, weights, heads, cols):
    cells, channels = normed.shape
    width = channels // heads
    smem = pl.BlockSpec(memory_space=pltpu.SMEM)
    whole = pl.BlockSpec((cells, channels), lambda i: (0, 0))
    column = pl.BlockSpec((channels, 2 * width), lambda i: (0, i))
    block = pl.BlockSpec((cells, 2 * width), lambda i: (0, i))
    shape = jax.ShapeDtypeStruct((cells, channels), BF16)
    return pl.pallas_call(
        functools.partial(attention_kernel, width, cols),
        grid=(heads // 2,),
        in_specs=[smem, smem, whole, whole, column, column, column]
        + [pl.BlockSpec((2 * width, channels), lambda i: (i, 0))],
        out_specs=[block] * 4,
        out_shape=[shape] * 4,
        compiler_params=pltpu.CompilerParams(vmem_limit_bytes=48 * 1024 * 1024),
        cost_estimate=pl.CostEstimate(
            flops=12 * cells * cells * channels + 8 * cells * channels * channels,
            bytes_accessed=16 * cells * channels,
            transcendentals=heads * cells * cells,
        ),
    )(ids, sizes, normed, grad_b, *weights)


def front_kernel(
    f_ref, g_ref, w_ref, ids_ref, sizes_ref, gain_ref,
    s_ref, gb_ref, pre_ref, hid_ref, norm_ref, valid_ref,
    grid, weight, w_sem, own_sem, y_send, y_recv, x_send, x_recv,
):
    count_y, count_x = lax.axis_size("sy"), lax.axis_size("sx")
    at_y, at_x = lax.axis_index("sy"), lax.axis_index("sx")
    rows_dev, cols_dev, width = f_ref.shape
    rows, cols = grid.shape[1:3]
    cells = rows * cols
    barrier = pltpu.get_barrier_semaphore()
    for step in range(1, count_y):
        pl.semaphore_signal(
            barrier, inc=1, device_id={"sy": lax.rem(at_y + step, count_y)}, device_id_type=MESH
        )
    for step in range(1, count_x):
        pl.semaphore_signal(
            barrier, inc=1, device_id={"sx": lax.rem(at_x + step, count_x)}, device_id_type=MESH
        )
    pl.semaphore_wait(barrier, count_y + count_x - 2)

    def tile(which, y):
        return grid.at[
            which,
            pl.ds(y * rows_dev, rows_dev),
            pl.ds(pl.multiple_of(at_x * cols_dev, cols_dev), cols_dev),
        ]

    fetch = pltpu.make_async_copy(w_ref, weight, w_sem)
    locals_, ups, acrosses = [], [[], []], [[], []]
    for which, ref in enumerate((f_ref, g_ref)):
        for step in range(1, count_y):
            copy = pltpu.make_async_remote_copy(
                src_ref=ref,
                dst_ref=tile(which, at_y),
                send_sem=y_send.at[which, step - 1],
                recv_sem=y_recv.at[which, step - 1],
                device_id={"sy": lax.rem(at_y + step, count_y)},
                device_id_type=MESH,
            )
            copy.start()
            ups[which].append(copy)
        own = pltpu.make_async_copy(ref, tile(which, at_y), own_sem.at[which])
        own.start()
        locals_.append(own)
    fetch.start()

    def across(which, back):
        y = lax.rem(at_y - back + count_y, count_y)
        for step in range(1, count_x):
            copy = pltpu.make_async_remote_copy(
                src_ref=(f_ref, g_ref)[which] if back == 0 else tile(which, y),
                dst_ref=tile(which, y),
                send_sem=x_send.at[which, back, step - 1],
                recv_sem=x_recv.at[which, back, step - 1],
                device_id={"sx": lax.rem(at_x + step, count_x)},
                device_id_type=MESH,
            )
            copy.start()
            acrosses[which].append(copy)

    across(0, 0)
    across(1, 0)
    for back in range(1, count_y):
        ups[0][back - 1].wait_recv()
        across(0, back)
    locals_[0].wait()
    for copy in acrosses[0]:
        copy.wait_recv()

    height, breadth = bucket_size(ids_ref, sizes_ref)
    edge = jnp.zeros((cols, width), BF16)
    for shift in range(3):
        s_ref[shift, 0:cols, :] = edge
        s_ref[shift, cells + cols : cells + 2 * cols, :] = edge

    def build(r, carry):
        at = pl.ds(pl.multiple_of(r * cols, cols), cols)
        to = pl.ds(pl.multiple_of((r + 1) * cols, cols), cols)
        column = lax.broadcasted_iota(jnp.int32, (cols, 1), 0)
        valid = (column < jnp.where(r < height, breadth, 0)).astype(F32)
        valid_ref[at, :] = valid
        line = grid[0, r].astype(F32) * valid
        zero = jnp.zeros((1, width), F32)
        s_ref[0, to, :] = jnp.concatenate([zero, line[:-1]], axis=0).astype(BF16)
        s_ref[1, to, :] = line.astype(BF16)
        s_ref[2, to, :] = jnp.concatenate([line[1:], zero], axis=0).astype(BF16)
        return carry

    lax.fori_loop(0, rows, build, 0)
    for back in range(1, count_y):
        ups[1][back - 1].wait_recv()
        across(1, back)
    fetch.wait()

    block = cells // 2

    def convolve(r, carry):
        total = None
        for t in range(9):
            dy, dx = t // 3, t % 3
            part = jnp.dot(
                s_ref[dx, pl.ds(pl.multiple_of(r * block + dy * cols, cols), block), :],
                weight[t * width : (t + 1) * width, :],
                preferred_element_type=F32,
            )
            total = part if total is None else total + part
        pre_ref[pl.ds(pl.multiple_of(r * block, block), block), :] = total
        return carry

    lax.fori_loop(0, 2, convolve, 0)
    locals_[1].wait()
    for copy in acrosses[1]:
        copy.wait_recv()

    gain = gain_ref[...].reshape(1, width)

    def finish(r, carry):
        at = pl.ds(pl.multiple_of(r * 2 * cols, cols), 2 * cols)
        valid = valid_ref[at, :]
        gb_ref[at, :] = (grid[1, pl.ds(2 * r, 2)].reshape(2 * cols, width).astype(F32) * valid).astype(BF16)
        pre = pre_ref[at, :]
        xin = s_ref[1, pl.ds(pl.multiple_of((2 * r + 1) * cols, cols), 2 * cols), :].astype(F32)
        hidden = (valid * (xin + pre * jax.nn.sigmoid(pre))).astype(BF16)
        hid_ref[at, :] = hidden
        hidden = hidden.astype(F32)
        centred = hidden - jnp.mean(hidden, axis=-1, keepdims=True)
        spread = jnp.mean(centred * centred, axis=-1, keepdims=True)
        norm_ref[at, :] = (centred * lax.rsqrt(spread + 1e-05) * gain).astype(BF16)
        return carry

    lax.fori_loop(0, rows // 2, finish, 0)
    for group in ups + acrosses:
        for copy in group:
            copy.wait_send()


def front(features, out_grad, conv_weight, ids, sizes, gain):
    count_y, count_x = lax.axis_size("sy"), lax.axis_size("sx")
    rows_dev, cols_dev, width = features.shape
    rows, cols = rows_dev * count_y, cols_dev * count_x
    cells = rows * cols
    vmem = pl.BlockSpec(memory_space=pltpu.VMEM)
    anywhere = pl.BlockSpec(memory_space=pl.ANY)
    smem = pl.BlockSpec(memory_space=pltpu.SMEM)
    dma = pltpu.SemaphoreType.DMA
    return pl.pallas_call(
        front_kernel,
        in_specs=[anywhere, anywhere, anywhere, smem, smem, vmem],
        out_specs=[vmem] * 6,
        out_shape=[
            jax.ShapeDtypeStruct((3, cells + 2 * cols, width), BF16),
            jax.ShapeDtypeStruct((cells, width), BF16),
            jax.ShapeDtypeStruct((cells, width), F32),
            jax.ShapeDtypeStruct((cells, width), BF16),
            jax.ShapeDtypeStruct((cells, width), BF16),
            jax.ShapeDtypeStruct((cells, 1), F32),
        ],
        scratch_shapes=[
            pltpu.VMEM((2, rows, cols, width), BF16),
            pltpu.VMEM(conv_weight.shape, BF16),
            dma,
            dma((2,)),
            dma((2, count_y - 1)),
            dma((2, count_y - 1)),
            dma((2, count_y, count_x - 1)),
            dma((2, count_y, count_x - 1)),
        ],
        compiler_params=pltpu.CompilerParams(
            collective_id=1, has_side_effects=True, vmem_limit_bytes=VMEM_LIMIT
        ),
    )(features, out_grad, conv_weight, ids, sizes, gain)


def back_kernel(
    share, n_ref, dq_ref, dk_ref, dv_ref, wq_ref, wk_ref, wv_ref, wo_ref,
    gb_ref, hid_ref, pre_ref, ctx_ref, valid_ref, gain_ref, s_ref,
    cv_out, gq_out, gk_out, gv_out, go_out, block_out,
    sq_ref, own, own_t, taps, cv, cv_pair, sq_pair, cv_sum, sq_sum, cv_got, sq_got,
    pair_send, pair_recv, far_send, far_recv,
):
    count = lax.axis_size("dp")
    half = count // 2
    me = lax.axis_index("dp")
    level, bit = me // 2, me % 2
    partner = me + 1 - 2 * bit
    at_y, at_x = lax.axis_index("sy"), lax.axis_index("sx")
    place = at_y * lax.axis_size("sx") + at_x
    cells, width = gb_ref.shape
    cols = s_ref.shape[1] - cells
    cols = cols // 2
    barrier = pltpu.get_barrier_semaphore()
    pl.semaphore_signal(barrier, inc=1, device_id={"dp": partner}, device_id_type=MESH)
    for step in range(1, half):
        pl.semaphore_signal(
            barrier,
            inc=1,
            device_id={"dp": 2 * lax.rem(level + step, half) + bit},
            device_id_type=MESH,
        )
    pl.semaphore_wait(barrier, half)

    order = list(range(1, half)) + [0]

    def to_partner(which, src, got):
        copies = {}
        for step in order:
            chunk = 2 * lax.rem(level + step, half) + 1 - bit
            copies[step] = pltpu.make_async_remote_copy(
                src_ref=src.at[chunk],
                dst_ref=got.at[step],
                send_sem=pair_send.at[which, step],
                recv_sem=pair_recv.at[which, step],
                device_id={"dp": partner},
                device_id_type=MESH,
            )
            copies[step].start()
        return copies

    def to_far(which, near, src, got, total, landed):
        copies = {}
        for step in order[:-1]:
            peer = 2 * lax.rem(level + step, half) + bit
            near[step].wait_recv()
            total[step - 1] = (src[peer].astype(F32) + got[step].astype(F32)).astype(BF16)
            copies[step] = pltpu.make_async_remote_copy(
                src_ref=total.at[step - 1],
                dst_ref=landed.at[step - 1],
                send_sem=far_send.at[which, step - 1],
                recv_sem=far_recv.at[which, step - 1],
                device_id={"dp": peer},
                device_id_type=MESH,
            )
            copies[step].start()
        return copies

    def collect(near, far, src, got, landed):
        near[0].wait_recv()
        value = src[me].astype(F32) + got[0].astype(F32)
        for step in order[:-1]:
            far[step].wait_recv()
            value += landed[step - 1].astype(F32)
        return value

    def own_columns(value):
        mine = value[:, 0:share]
        for index in range(1, width // share):
            mine = jnp.where(place == index, value[:, index * share : (index + 1) * share], mine)
        return mine

    dthree = [own_columns(ref[...]) for ref in (dq_ref, dk_ref, dv_ref)]
    normed_t = n_ref[...].T
    context_t = ctx_ref[...].reshape(cells, width).T
    made = [jnp.dot(normed_t, part, preferred_element_type=F32) for part in dthree]
    made.append(jnp.dot(context_t, own_columns(gb_ref[...]), preferred_element_type=F32))
    made = jnp.concatenate(made, axis=1)
    lines = width // count
    for index in range(count):
        sq_ref[index] = made[index * lines : (index + 1) * lines].astype(BF16)
    sq_near = to_partner(0, sq_ref, sq_pair)

    rows_at = cells // 4

    def backward(r, carry):
        at = pl.ds(pl.multiple_of(r * rows_at, rows_at), rows_at)
        dnormed = dot_t(dq_ref[at, :], wq_ref[...], 1, 1)
        dnormed += dot_t(dk_ref[at, :], wk_ref[...], 1, 1)
        dnormed += dot_t(dv_ref[at, :], wv_ref[...], 1, 1)
        hidden = hid_ref[at, :].astype(F32)
        centred = hidden - jnp.mean(hidden, axis=-1, keepdims=True)
        spread = jnp.mean(centred * centred, axis=-1, keepdims=True)
        rstd = lax.rsqrt(spread + 1e-05)
        unit = centred * rstd
        up = dnormed * gain_ref[...].reshape(1, width)
        down = up - jnp.mean(up, axis=-1, keepdims=True)
        down = rstd * (down - unit * jnp.mean(up * unit, axis=-1, keepdims=True))
        pre = pre_ref[at, :]
        sig = jax.nn.sigmoid(pre)
        dpre = (gb_ref[at, :].astype(F32) + down) * sig * (1.0 + pre * (1.0 - sig))
        dpre = dpre * valid_ref[at, :]
        own[at, :] = own_columns(dpre)
        return carry

    lax.fori_loop(0, 4, backward, 0)
    sq_far = to_far(0, sq_near, sq_ref, sq_pair, sq_sum, sq_got)
    own_t[...] = own[...].T.astype(BF16)
    for t in range(9):
        dy, dx = t // 3, t % 3
        taps[:, t * width : (t + 1) * width] = jnp.dot(
            own_t[...],
            s_ref[dx, dy * cols : dy * cols + cells, :],
            preferred_element_type=F32,
        )
    piece = taps.shape[1] // count
    spare = jnp.zeros((share, cv.shape[2] - piece), F32)
    for index in range(count):
        part = taps[:, index * piece : (index + 1) * piece]
        cv[index] = jnp.concatenate([part, spare], axis=1).astype(BF16)
    cv_near = to_partner(1, cv, cv_pair)

    rows_dev, cols_dev = block_out.shape[:2]
    rows_own = pl.ds(at_y * rows_dev, rows_dev)
    cols_own = pl.ds(pl.multiple_of(at_x * cols_dev, cols_dev), cols_dev)
    context = ctx_ref[rows_own, cols_own, :].reshape(rows_dev * cols_dev, width)
    made = jnp.dot(context, wo_ref[...], preferred_element_type=F32)
    for r in range(rows_dev):
        start = pl.multiple_of((at_y * rows_dev + r) * cols + at_x * cols_dev, cols_dev)
        line = pl.ds(start, cols_dev)
        value = hid_ref[line, :].astype(F32) + made[r * cols_dev : (r + 1) * cols_dev]
        block_out[r] = (value * valid_ref[line, :]).astype(BF16)

    cv_far = to_far(1, cv_near, cv, cv_pair, cv_sum, cv_got)
    squares = collect(sq_near, sq_far, sq_ref, sq_pair, sq_got)
    for index, ref in enumerate((gq_out, gk_out, gv_out, go_out)):
        ref[...] = squares[:, index * share : (index + 1) * share]
    cv_out[...] = collect(cv_near, cv_far, cv, cv_pair, cv_got)[:, :piece].T
    for group in (sq_near, sq_far, cv_near, cv_far):
        for copy in group.values():
            copy.wait_send()


def back(share, tile_shape, normed, arrays, context_grid, valid, gain, stack, piece):
    count = lax.axis_size("dp")
    half = count // 2
    cells, width = arrays[0].shape
    lanes = -(-piece // 128) * 128
    vmem = pl.BlockSpec(memory_space=pltpu.VMEM)
    dma = pltpu.SemaphoreType.DMA
    conv_shape, square_shape = (share, lanes), (width // count, 4 * share)
    return pl.pallas_call(
        functools.partial(back_kernel, share),
        in_specs=[vmem] * 15,
        out_specs=[vmem] * 6,
        out_shape=[
            jax.ShapeDtypeStruct((piece, share), F32),
            *[jax.ShapeDtypeStruct((width // count, share), F32)] * 4,
            jax.ShapeDtypeStruct(tile_shape, BF16),
        ],
        scratch_shapes=[
            pltpu.VMEM((count,) + square_shape, BF16),
            pltpu.VMEM((cells, share), F32),
            pltpu.VMEM((share, cells), BF16),
            pltpu.VMEM((share, 9 * width), F32),
            pltpu.VMEM((count,) + conv_shape, BF16),
            pltpu.VMEM((half,) + conv_shape, BF16),
            pltpu.VMEM((half,) + square_shape, BF16),
            pltpu.VMEM((half - 1,) + conv_shape, BF16),
            pltpu.VMEM((half - 1,) + square_shape, BF16),
            pltpu.VMEM((half - 1,) + conv_shape, BF16),
            pltpu.VMEM((half - 1,) + square_shape, BF16),
            dma((2, half)),
            dma((2, half)),
            dma((2, half - 1)),
            dma((2, half - 1)),
        ],
        compiler_params=pltpu.CompilerParams(
            collective_id=2, has_side_effects=True, vmem_limit_bytes=VMEM_LIMIT
        ),
    )(normed, *arrays, context_grid, valid, gain, stack)


def body(
    features,
    bucket_ids,
    bucket_sizes,
    conv_weight,
    norm_gain,
    query_weight,
    key_weight,
    value_weight,
    out_weight,
    out_grad,
):
    rows_dev, cols_dev, width = features.shape[1:]
    count_y = lax.axis_size("sy")
    count_x = lax.axis_size("sx")
    count_d = lax.axis_size("dp")
    rows, cols = rows_dev * count_y, cols_dev * count_x
    share = width // (count_y * count_x)
    piece = conv_weight.shape[0] // count_d
    stack, grad_b, pre, hidden, normed, valid = front(
        features[0], out_grad[0], conv_weight, bucket_ids, bucket_sizes, norm_gain
    )
    weights = (query_weight, key_weight, value_weight, out_weight)
    context, dquery, dkey, dvalue = attention(
        bucket_ids, bucket_sizes, normed, grad_b, weights, HEADS, cols
    )
    *grads, block = back(
        share,
        features.shape[1:],
        normed,
        (dquery, dkey, dvalue, *weights, grad_b, hidden, pre),
        context.reshape(rows, cols, width),
        valid,
        norm_gain,
        stack,
        piece,
    )
    return (block[None], *grads)


def solution(mesh):
    placed = (
        P("dp", "sy", "sx", None),
        P("dp"),
        P(),
        P(),
        P(),
        P(),
        P(),
        P(),
        P(),
        P("dp", "sy", "sx", None),
    )
    return jax.shard_map(
        body,
        mesh=mesh,
        in_specs=placed,
        out_specs=(
            P("dp", "sy", "sx", None),
            P("dp", ("sy", "sx")),
            P("dp", ("sy", "sx")),
            P("dp", ("sy", "sx")),
            P("dp", ("sy", "sx")),
            P("dp", ("sy", "sx")),
        ),
        check_vma=False,
    )
```
